32 devices in a mesh: ang: 8 (over z, core), col: 4 (over y, x).
Axes of the slice: x: 2, y: 2, z: 4, core: 2. Of those that a mesh axis runs over, the one named last changes fastest.
Arguments:
- projections: float32 [512, 16, 4096], P('ang', None, 'col'), may hold values from -6 to 6
- margin: int32 [16], replicated, may hold values from 128 to 384, as said below
- ramp_length: int32 [16], replicated, may hold values from 32 to 128, as said below
Outputs:
- smoothed: float32 [512, 16, 4096], P('ang', None, 'col')
The draws below stay inside these ranges and needn't reach their ends.
Inputs may be any that keep to these rules, and one draw needn't show every extreme that they name: `margin`: one row has exactly 384 and another exactly 128; other rows may repeat values. `ramp_length`: one row has exactly 128; other rows may repeat values.
All inputs are finite; a program needn't handle non-finite values.
Results may differ from the reference program's by a relative error of at most 0.0003.
Values sent between devices are 32-bit elements; how exact they have to be, the bound alone decides.
A program may use at most 64 MiB of HBM per device.

```python
import jax
import jax.numpy as jnp
from jax import lax

DET_COLS = 4096
DET_ROWS = 16
BAND_MAX = 384
RAMP_MAX = 128
DIFF_STEPS = 6
VIEWS = 512


def draw_margin(key, part):
    first_key, second_key = jax.random.split(jax.random.fold_in(key, 11))
    values = jax.random.randint(first_key, (DET_ROWS,), RAMP_MAX, BAND_MAX + 1)
    order = jax.random.permutation(second_key, DET_ROWS)
    values = values.at[order[0]].set(BAND_MAX).at[order[1]].set(RAMP_MAX)
    return values.astype(jnp.int32)


def draw_ramp_length(key, part):
    first_key, second_key = jax.random.split(jax.random.fold_in(key, 23))
    values = jax.random.randint(first_key, (DET_ROWS,), RAMP_MAX // 4, RAMP_MAX + 1)
    order = jax.random.permutation(second_key, DET_ROWS)
    values = values.at[order[0]].set(RAMP_MAX)
    return values.astype(jnp.int32)


def block_scale(key, extent, cuts, low, high):
    def one(dim, blocks):
        steps = jax.random.uniform(jax.random.fold_in(jax.random.fold_in(key, 6), dim), (blocks,), jnp.float32, low / len(cuts), high / len(cuts))
        return jnp.repeat(jnp.exp(steps), extent[dim] // blocks).reshape((-1,) + (1,) * (len(extent) - dim - 1))

    factor_of = one(*cuts[0])
    for cut in cuts[1:]:
        factor_of = factor_of * one(*cut)
    return factor_of


def noise(rng, shape, scale, reach, cuts=(), held_as=jnp.bfloat16):
    drawn = jax.random.normal(rng, shape, jnp.float32) * scale
    if len(cuts) > 0:
        drawn = block_scale(rng, shape, cuts, -0.22, 0.18) * drawn
    return jnp.clip(drawn, min=-reach, max=reach).astype(held_as)


def setup_inputs(seed: int = 0) -> dict:
    streams_of = jax.random.split(jax.random.key(seed), 4)
    projections = noise(streams_of[0], (VIEWS, DET_ROWS, DET_COLS), 1.0, 6.0, ((0, 8), (2, 4)), jnp.float32)
    margin = draw_margin(jax.random.fold_in(streams_of[3], 71), 0)
    ramp_length = draw_ramp_length(jax.random.fold_in(streams_of[3], 71), 0)
    return {"projections": projections, "margin": margin, "ramp_length": ramp_length}


time_step = 0.2
edge_scale = 0.8


def conductive_flux(delta):
    return delta / (1.0 + (delta / edge_scale) * (delta / edge_scale))


def diffuse_plane(field_now, half_turn):
    prior_view = jnp.roll(field_now, 1, axis=0)
    next_view = jnp.roll(field_now, -1, axis=0)
    flipped = jnp.roll(field_now, -half_turn, axis=0)
    inward = jnp.concatenate([flipped[:, :1], field_now[:, :-1]], axis=1)
    outward = jnp.concatenate([field_now[:, 1:], field_now[:, -1:]], axis=1)
    summed = conductive_flux(prior_view - field_now) + conductive_flux(next_view - field_now)
    summed = summed + conductive_flux(inward - field_now)
    summed = summed + conductive_flux(outward - field_now)
    return field_now + time_step * summed


def reference(projections, margin, ramp_length):
    half_turn = projections.shape[0] // 2
    columns = jnp.arange(DET_COLS, dtype=jnp.int32)
    position = columns.astype(jnp.float32)

    def one_row(row_inputs):
        detector_plane, shift_cols, ramp_cols = row_inputs
        direct_index = jnp.minimum(columns + shift_cols, DET_COLS - 1).astype(jnp.int32)
        direct = detector_plane[:, direct_index]
        mirror_index = jnp.clip(shift_cols - 1 - columns, 0, DET_COLS - 1).astype(jnp.int32)
        partner = jnp.roll(detector_plane, -half_turn, axis=0)
        mirror = partner[:, mirror_index]
        mirror = jnp.where((shift_cols - 1 - columns)[None, :] >= 0, mirror, 0.0)
        spread = 2.0 * ramp_cols.astype(jnp.float32)
        weight = jnp.minimum(1.0, 0.5 + (position + 0.5) / spread)
        field_now = weight[None, :] * direct + (1.0 - weight)[None, :] * mirror
        for step_index in range(DIFF_STEPS):
            field_now = diffuse_plane(field_now, half_turn)
        return field_now

    planes = lax.map(one_row, (jnp.moveaxis(projections, 1, 0), margin, ramp_length))
    return jnp.moveaxis(planes, 0, 1)
```

```python
import functools

import jax
import jax.numpy as jnp
from jax import lax
from jax.experimental import pallas as pl
from jax.experimental.pallas import tpu as pltpu
from jax.sharding import PartitionSpec as P

BAND = 384
STEPS = 6
LANES = 128
BAND_BLOCKS = BAND // LANES
TIME_STEP = 0.2
EDGE_SCALE = 0.8
SCALE = (1.0 / TIME_STEP) ** 0.5 / EDGE_SCALE
MESH = pl.DeviceIdType.MESH
VMEM_LIMIT = 56 * 1024 * 1024


def take_lanes(block, index):
    return jnp.take_along_axis(block, index, axis=1)


def align_kernel(margin_ref, data_ref, row_ref, band_ref, rim_ref):
    views, rows, width = data_ref.shape
    count = width // LANES
    is_last = lax.axis_index("col") == lax.axis_size("col") - 1
    lane = lax.broadcasted_iota(jnp.int32, (8, LANES), 1)
    sublane = lax.broadcasted_iota(jnp.int32, (8, LANES), 0)
    limit = jnp.where(is_last, width, 2 * width)

    def one_view(v, _):
        rim = jnp.zeros((8, LANES), jnp.float32)
        for h in range(rows // 8):
            rs = pl.ds(8 * h, 8)
            margin = margin_ref[rs, :]
            turn = (lane + margin) & (LANES - 1)
            stay = lane + (margin & (LANES - 1)) < LANES
            blocks_on = margin >> 7
            raw = [data_ref[v, rs, pl.ds(LANES * k, LANES)] for k in range(count)]
            turned = [take_lanes(b, turn) for b in raw]
            joined = [jnp.where(stay, turned[k], turned[(k + 1) % count]) for k in range(count)]
            rolled = [
                jnp.where(
                    blocks_on == 1,
                    joined[(k + 1) % count],
                    jnp.where(blocks_on == 2, joined[(k + 2) % count], joined[(k + 3) % count]),
                )
                for k in range(count)
            ]
            edge = take_lanes(raw[-1], jnp.full((8, LANES), LANES - 1, jnp.int32))
            for k in range(count):
                kept = rolled[k]
                if k >= count - BAND_BLOCKS:
                    band_ref[v, rs, pl.ds(LANES * (k - count + BAND_BLOCKS), LANES)] = kept
                    kept = jnp.where(lane + LANES * k + margin < limit, kept, edge)
                row_ref[v, rs, pl.ds(LANES * k, LANES)] = kept
            row_ref[v, rs, pl.ds(width, LANES)] = jnp.where(
                jnp.logical_and(is_last, lane < LANES // 2), edge, rolled[-1]
            )
            head = take_lanes(rolled[0], lane & 7)
            rim = rim + jnp.where((lane >> 3) == sublane + 8 * h, head, 0.0)
        rim_ref[v] = jnp.sum(rim, axis=0, keepdims=True)
        return 0

    lax.fori_loop(0, views, one_view, 0)


def exchange_kernel(
    row_ref, band_ref, rim_ref,
    low_ref, high_ref, next_ref, mirror_ref, right_ref, facing_ref,
    send_sem, recv_sem,
):
    views = row_ref.shape[0]
    ang, col = lax.axis_index("ang"), lax.axis_index("col")
    n_ang, n_col = lax.axis_size("ang"), lax.axis_size("col")
    half = n_ang // 2
    d = STEPS
    up, down = lax.rem(ang + 1, n_ang), lax.rem(ang + n_ang - 1, n_ang)
    across = lax.rem(ang + half, n_ang)
    across_up, across_down = lax.rem(ang + half + 1, n_ang), lax.rem(ang + half - 1, n_ang)
    prev = jnp.maximum(col - 1, 0)
    after = jnp.minimum(col + 1, n_col - 1)
    has_prev, has_next, at_axis = col > 0, col < n_col - 1, col == 0

    barrier = pltpu.get_barrier_semaphore()

    def greet(a, c):
        pl.semaphore_signal(barrier, inc=1, device_id=(a, c), device_id_type=MESH)

    greet(up, col)
    greet(down, col)

    @pl.when(has_prev)
    def _():
        for a in (ang, up, down):
            greet(a, prev)

    @pl.when(has_next)
    def _():
        for a in (ang, up, down):
            greet(a, after)

    @pl.when(at_axis)
    def _():
        for a in (across, across_up, across_down):
            greet(a, col)

    peers = 2
    for present in (has_prev, has_next, at_axis):
        peers = peers + 3 * present.astype(jnp.int32)
    pl.semaphore_wait(barrier, peers)

    used = [0]

    def copy(src, dst, a, c):
        i = used[0]
        used[0] += 1
        return pltpu.make_async_remote_copy(
            src_ref=src, dst_ref=dst, send_sem=send_sem.at[i], recv_sem=recv_sem.at[i],
            device_id=(a, c), device_id_type=MESH,
        )

    first, last, whole = pl.ds(0, d), pl.ds(views - d, d), pl.ds(0, views)
    low_end, high_end, middle = pl.ds(0, d), pl.ds(views + d, d), pl.ds(d, views)
    tail = pl.ds(BAND - LANES, LANES)

    band_edges = [
        copy(band_ref.at[first], next_ref.at[pl.ds(d, d)], ang, prev),
        copy(band_ref.at[last], next_ref.at[pl.ds(views, d)], ang, prev),
    ]
    inner = views - 2 * d
    band_inner = [copy(band_ref.at[pl.ds(d, inner)], next_ref.at[pl.ds(2 * d, inner)], ang, prev)]
    rims = [
        copy(rim_ref.at[whole], right_ref.at[middle], ang, prev),
        copy(rim_ref.at[first], right_ref.at[high_end], down, prev),
        copy(rim_ref.at[last], right_ref.at[low_end], up, prev),
    ]
    mirrors = [
        copy(rim_ref.at[whole], facing_ref.at[middle], across, col),
        copy(rim_ref.at[first], facing_ref.at[high_end], across_down, col),
        copy(rim_ref.at[last], facing_ref.at[low_end], across_up, col),
        copy(band_ref.at[first, :, tail], mirror_ref.at[high_end], across_down, col),
        copy(band_ref.at[last, :, tail], mirror_ref.at[low_end], across_up, col),
        copy(band_ref.at[whole, :, tail], mirror_ref.at[middle], across, col),
    ]
    turns = [
        copy(row_ref.at[first], high_ref, down, col),
        copy(row_ref.at[last], low_ref, up, col),
    ]
    passed_on = [
        copy(next_ref.at[pl.ds(d, d)], next_ref.at[high_end], down, col),
        copy(next_ref.at[pl.ds(views, d)], next_ref.at[low_end], up, col),
    ]
    leftward = band_edges + rims + band_inner

    @pl.when(has_prev)
    def _():
        for c in leftward:
            c.start()

    @pl.when(at_axis)
    def _():
        for c in mirrors:
            c.start()

    for c in turns:
        c.start()

    @pl.when(has_next)
    def _():
        for c in band_edges:
            c.wait_recv()
        for c in passed_on:
            c.start()
        for c in rims + band_inner:
            c.wait_recv()
        for c in passed_on:
            c.wait()

    @pl.when(at_axis)
    def _():
        for c in mirrors:
            c.wait()

    for c in turns:
        c.wait()

    @pl.when(has_prev)
    def _():
        for c in leftward:
            c.wait_send()


def flux(delta):
    return delta * pl.reciprocal(5.0 + delta * delta, approx=True)


def diffuse_kernel(
    margin_ref, ramp_ref, row_ref, low_ref, high_ref, next_ref, mirror_ref, right_ref, facing_ref,
    out_ref, field,
):
    views, rows, reach = row_ref.shape
    width = reach - LANES
    count = width // LANES
    d = STEPS
    is_last = lax.axis_index("col") == lax.axis_size("col") - 1
    is_first = lax.axis_index("col") == 0
    lane = lax.broadcasted_iota(jnp.int32, (8, LANES), 1)
    sublane = lax.broadcasted_iota(jnp.int32, (8, LANES), 0)
    limit = jnp.where(is_last, 4 * width, width)

    def weight_of(position, spread):
        return jnp.clip(0.5 + (position.astype(jnp.float32) + 0.5) / spread, 0.0, 1.0)

    def stitch(source_ref, offset, length, h):
        rs = pl.ds(8 * h, 8)
        margin = margin_ref[rs, :]
        spread = 2.0 * ramp_ref[rs, :].astype(jnp.float32)
        head = weight_of(lane, spread)
        inner = weight_of(lane - LANES, spread)
        cell = (sublane + 8 * h) * 8

        def one(i, _):
            p = i + offset
            for k in range(1, count):
                block = source_ref[i, rs, pl.ds(LANES * k, LANES)]
                j = k - count + BAND_BLOCKS
                if j >= 0:
                    following = next_ref[p, rs, pl.ds(LANES * j, LANES)]
                    block = jnp.where(lane + LANES * k + margin < limit, block, following)
                field[p, rs, pl.ds(LANES * k, LANES)] = SCALE * block
            block = source_ref[i, rs, pl.ds(0, LANES)]
            facing = take_lanes(mirror_ref[p, rs, :], LANES - 1 - lane)
            blended = head * block + (1.0 - head) * facing
            field[p, rs, pl.ds(0, LANES)] = SCALE * jnp.where(is_first, blended, block)
            block = source_ref[i, rs, pl.ds(width, LANES)]
            facing = take_lanes(jnp.broadcast_to(facing_ref[p], (8, LANES)), cell + ((LANES - 1 - lane) & 7))
            blended = inner * block + (1.0 - inner) * facing
            inward = jnp.where(is_first, blended, block)
            outward = take_lanes(jnp.broadcast_to(right_ref[p], (8, LANES)), cell + (lane & 7))
            outward = jnp.where(is_last, block, outward)
            field[p, rs, pl.ds(width, LANES)] = SCALE * jnp.where(lane < LANES // 2, outward, inward)
            return 0

        lax.fori_loop(0, length, one, 0)

    for h in range(rows // 8):
        stitch(low_ref, 0, d, h)
        stitch(row_ref, d, views, h)
        stitch(high_ref, views + d, d, h)

    for step in range(1, STEPS + 1):
        for h in range(rows // 8):
            rs = pl.ds(8 * h, 8)

            def one(v, carried):
                current, before = carried
                later = field[v + 1, rs, :]
                ahead = flux(later - current)
                outward = flux(pltpu.roll(current, reach - 1, 1) - current)
                inward = pltpu.roll(outward, 1, 1)
                updated = current + ((ahead - before) + (outward - inward))
                if step < STEPS:
                    field[v, rs, :] = updated
                else:
                    out_ref[v - d, rs, :] = updated[:, :width] * (1.0 / SCALE)
                return later, ahead

            current = field[step, rs, :]
            before = flux(current - field[step - 1, rs, :])
            lax.fori_loop(step, views + 2 * d - step, one, (current, before))


def per_device(projections, margin, ramp_length):
    views, rows, width = projections.shape
    margin = jnp.broadcast_to(margin[:, None], (rows, LANES))
    ramp = jnp.broadcast_to(ramp_length[:, None], (rows, LANES))
    tall = views + 2 * STEPS
    reach = width + LANES
    f32 = jnp.float32
    shape = jax.ShapeDtypeStruct
    vmem = pl.BlockSpec(memory_space=pltpu.VMEM)
    anywhere = pl.BlockSpec(memory_space=pl.ANY)
    row, band, rim = pl.pallas_call(
        align_kernel,
        out_shape=(
            shape((views, rows, reach), f32),
            shape((views, rows, BAND), f32),
            shape((views, 1, LANES), f32),
        ),
        in_specs=[vmem] * 2,
        out_specs=(vmem,) * 3,
        compiler_params=pltpu.CompilerParams(vmem_limit_bytes=VMEM_LIMIT),
    )(margin, projections)
    parts = pl.pallas_call(
        exchange_kernel,
        out_shape=(
            shape((STEPS, rows, reach), f32),
            shape((STEPS, rows, reach), f32),
            shape((tall, rows, BAND), f32),
            shape((tall, rows, LANES), f32),
            shape((tall, 1, LANES), f32),
            shape((tall, 1, LANES), f32),
        ),
        in_specs=[anywhere] * 3,
        out_specs=(anywhere,) * 6,
        scratch_shapes=[pltpu.SemaphoreType.DMA((16,)), pltpu.SemaphoreType.DMA((16,))],
        compiler_params=pltpu.CompilerParams(collective_id=0, has_side_effects=True),
    )(row, band, rim)
    return pl.pallas_call(
        diffuse_kernel,
        out_shape=shape((views, rows, width), f32),
        in_specs=[vmem] * 9,
        out_specs=vmem,
        scratch_shapes=[pltpu.VMEM((tall, rows, reach), f32)],
        compiler_params=pltpu.CompilerParams(vmem_limit_bytes=VMEM_LIMIT),
    )(margin, ramp, row, *parts)


def solution(mesh):
    in_specs = (P("ang", None, "col"), P(), P())
    out_specs = P("ang", None, "col")
    return jax.shard_map(
        per_device, mesh=mesh, in_specs=in_specs, out_specs=out_specs, check_vma=False
    )
```

```python
import functools

import jax
import jax.numpy as jnp
from jax import lax
from jax.experimental import pallas as pl
from jax.experimental.pallas import tpu as pltpu
from jax.sharding import PartitionSpec as P

BAND = 384
STEPS = 6
LANES = 128
BAND_BLOCKS = BAND // LANES
TIME_STEP = 0.2
EDGE_SCALE = 0.8
SCALE = (1.0 / TIME_STEP) ** 0.5 / EDGE_SCALE
MESH = pl.DeviceIdType.MESH
VMEM_LIMIT = 56 * 1024 * 1024
VIEWS_AT_ONCE = 4
ROWS_AT_ONCE = 16
UNROLL = 4


def take_lanes(block, index):
    return jnp.take_along_axis(block, index, axis=1)


def align_kernel(margin_ref, data_ref, row_ref, band_ref, rim_ref):
    views, rows, width = data_ref.shape
    count = width // LANES
    is_last = lax.axis_index("col") == lax.axis_size("col") - 1
    lane = lax.broadcasted_iota(jnp.int32, (8, LANES), 1)
    sublane = lax.broadcasted_iota(jnp.int32, (8, LANES), 0)
    limit = jnp.where(is_last, width, 2 * width)

    def one_view(v, _):
        rim = jnp.zeros((8, LANES), jnp.float32)
        for h in range(rows // 8):
            rs = pl.ds(8 * h, 8)
            margin = margin_ref[rs, :]
            turn = (lane + margin) & (LANES - 1)
            stay = lane + (margin & (LANES - 1)) < LANES
            blocks_on = margin >> 7
            raw = [data_ref[v, rs, pl.ds(LANES * k, LANES)] for k in range(count)]
            turned = [take_lanes(b, turn) for b in raw]
            joined = [jnp.where(stay, turned[k], turned[(k + 1) % count]) for k in range(count)]
            rolled = [
                jnp.where(
                    blocks_on == 1,
                    joined[(k + 1) % count],
                    jnp.where(blocks_on == 2, joined[(k + 2) % count], joined[(k + 3) % count]),
                )
                for k in range(count)
            ]
            edge = take_lanes(raw[-1], jnp.full((8, LANES), LANES - 1, jnp.int32))
            for k in range(count):
                kept = rolled[k]
                if k >= count - BAND_BLOCKS:
                    band_ref[v, rs, pl.ds(LANES * (k - count + BAND_BLOCKS), LANES)] = kept
                    kept = jnp.where(lane + LANES * k + margin < limit, kept, edge)
                row_ref[v, rs, pl.ds(LANES * k, LANES)] = kept
            row_ref[v, rs, pl.ds(width, LANES)] = jnp.where(
                jnp.logical_and(is_last, lane < LANES // 2), edge, rolled[-1]
            )
            head = take_lanes(rolled[0], lane & 7)
            rim = rim + jnp.where((lane >> 3) == sublane + 8 * h, head, 0.0)
        rim_ref[v] = jnp.sum(rim, axis=0, keepdims=True)
        return 0

    lax.fori_loop(0, views, one_view, 0, unroll=UNROLL)


def exchange_kernel(
    row_ref, band_ref, rim_ref,
    low_ref, high_ref, next_ref, mirror_ref, right_ref, facing_ref,
    send_sem, recv_sem,
):
    views = row_ref.shape[0]
    ang, col = lax.axis_index("ang"), lax.axis_index("col")
    n_ang, n_col = lax.axis_size("ang"), lax.axis_size("col")
    half = n_ang // 2
    d = STEPS
    up, down = lax.rem(ang + 1, n_ang), lax.rem(ang + n_ang - 1, n_ang)
    across = lax.rem(ang + half, n_ang)
    across_up, across_down = lax.rem(ang + half + 1, n_ang), lax.rem(ang + half - 1, n_ang)
    prev = jnp.maximum(col - 1, 0)
    after = jnp.minimum(col + 1, n_col - 1)
    has_prev, has_next, at_axis = col > 0, col < n_col - 1, col == 0

    barrier = pltpu.get_barrier_semaphore()

    def greet(a, c):
        pl.semaphore_signal(barrier, inc=1, device_id=(a, c), device_id_type=MESH)

    greet(up, col)
    greet(down, col)

    @pl.when(has_prev)
    def _():
        for a in (ang, up, down):
            greet(a, prev)

    @pl.when(has_next)
    def _():
        for a in (ang, up, down):
            greet(a, after)

    @pl.when(at_axis)
    def _():
        for a in (across, across_up, across_down):
            greet(a, col)

    peers = 2
    for present in (has_prev, has_next, at_axis):
        peers = peers + 3 * present.astype(jnp.int32)
    pl.semaphore_wait(barrier, peers)

    used = [0]

    def copy(src, dst, a, c):
        i = used[0]
        used[0] += 1
        return pltpu.make_async_remote_copy(
            src_ref=src, dst_ref=dst, send_sem=send_sem.at[i], recv_sem=recv_sem.at[i],
            device_id=(a, c), device_id_type=MESH,
        )

    first, last, whole = pl.ds(0, d), pl.ds(views - d, d), pl.ds(0, views)
    low_end, high_end, middle = pl.ds(0, d), pl.ds(views + d, d), pl.ds(d, views)
    tail = pl.ds(BAND - LANES, LANES)

    band_edges = [
        copy(band_ref.at[first], next_ref.at[pl.ds(d, d)], ang, prev),
        copy(band_ref.at[last], next_ref.at[pl.ds(views, d)], ang, prev),
    ]
    inner = views - 2 * d
    band_inner = [copy(band_ref.at[pl.ds(d, inner)], next_ref.at[pl.ds(2 * d, inner)], ang, prev)]
    rims = [
        copy(rim_ref.at[whole], right_ref.at[middle], ang, prev),
        copy(rim_ref.at[first], right_ref.at[high_end], down, prev),
        copy(rim_ref.at[last], right_ref.at[low_end], up, prev),
    ]
    mirrors = [
        copy(rim_ref.at[whole], facing_ref.at[middle], across, col),
        copy(rim_ref.at[first], facing_ref.at[high_end], across_down, col),
        copy(rim_ref.at[last], facing_ref.at[low_end], across_up, col),
        copy(band_ref.at[first, :, tail], mirror_ref.at[high_end], across_down, col),
        copy(band_ref.at[last, :, tail], mirror_ref.at[low_end], across_up, col),
        copy(band_ref.at[whole, :, tail], mirror_ref.at[middle], across, col),
    ]
    turns = [
        copy(row_ref.at[first], high_ref, down, col),
        copy(row_ref.at[last], low_ref, up, col),
    ]
    passed_on = [
        copy(next_ref.at[pl.ds(d, d)], next_ref.at[high_end], down, col),
        copy(next_ref.at[pl.ds(views, d)], next_ref.at[low_end], up, col),
    ]
    leftward = band_edges + rims + band_inner

    @pl.when(has_prev)
    def _():
        for c in leftward:
            c.start()

    @pl.when(at_axis)
    def _():
        for c in mirrors:
            c.start()

    for c in turns:
        c.start()

    @pl.when(has_next)
    def _():
        for c in band_edges:
            c.wait_recv()
        for c in passed_on:
            c.start()
        for c in rims + band_inner:
            c.wait_recv()
        for c in passed_on:
            c.wait()

    @pl.when(at_axis)
    def _():
        for c in mirrors:
            c.wait()

    for c in turns:
        c.wait()

    @pl.when(has_prev)
    def _():
        for c in leftward:
            c.wait_send()


def flux(delta):
    return delta * pl.reciprocal(5.0 + delta * delta, approx=True)


def diffuse_kernel(
    margin_ref, ramp_ref, row_ref, low_ref, high_ref, next_ref, mirror_ref, right_ref, facing_ref,
    out_ref, field,
):
    views, rows, reach = row_ref.shape
    width = reach - LANES
    count = width // LANES
    d = STEPS
    is_last = lax.axis_index("col") == lax.axis_size("col") - 1
    is_first = lax.axis_index("col") == 0
    lane = lax.broadcasted_iota(jnp.int32, (8, LANES), 1)
    sublane = lax.broadcasted_iota(jnp.int32, (8, LANES), 0)
    limit = jnp.where(is_last, 4 * width, width)

    def weight_of(position, spread):
        return jnp.clip(0.5 + (position.astype(jnp.float32) + 0.5) / spread, 0.0, 1.0)

    def stitch(source_ref, offset, length, h):
        rs = pl.ds(8 * h, 8)
        margin = margin_ref[rs, :]
        spread = 2.0 * ramp_ref[rs, :].astype(jnp.float32)
        head = weight_of(lane, spread)
        inner = weight_of(lane - LANES, spread)
        cell = (sublane + 8 * h) * 8

        def one(i, _):
            p = i + offset
            for k in range(1, count):
                block = source_ref[i, rs, pl.ds(LANES * k, LANES)]
                j = k - count + BAND_BLOCKS
                if j >= 0:
                    following = next_ref[p, rs, pl.ds(LANES * j, LANES)]
                    block = jnp.where(lane + LANES * k + margin < limit, block, following)
                field[p, rs, pl.ds(LANES * k, LANES)] = SCALE * block
            block = source_ref[i, rs, pl.ds(0, LANES)]
            facing = take_lanes(mirror_ref[p, rs, :], LANES - 1 - lane)
            blended = head * block + (1.0 - head) * facing
            field[p, rs, pl.ds(0, LANES)] = SCALE * jnp.where(is_first, blended, block)
            block = source_ref[i, rs, pl.ds(width, LANES)]
            facing = take_lanes(jnp.broadcast_to(facing_ref[p], (8, LANES)), cell + ((LANES - 1 - lane) & 7))
            blended = inner * block + (1.0 - inner) * facing
            inward = jnp.where(is_first, blended, block)
            outward = take_lanes(jnp.broadcast_to(right_ref[p], (8, LANES)), cell + (lane & 7))
            outward = jnp.where(is_last, block, outward)
            field[p, rs, pl.ds(width, LANES)] = SCALE * jnp.where(lane < LANES // 2, outward, inward)
            return 0

        lax.fori_loop(0, length, one, 0, unroll=2)

    for h in range(rows // 8):
        stitch(low_ref, 0, d, h)
        stitch(row_ref, d, views, h)
        stitch(high_ref, views + d, d, h)

    slabs = range(0, rows, ROWS_AT_ONCE)
    for step in range(1, STEPS + 1):
        for first_row in slabs:
            rs = pl.ds(first_row, ROWS_AT_ONCE)

            def some(i, carried):
                current, before = carried
                v = step + i * VIEWS_AT_ONCE
                loaded = [field[v + 1 + u, rs, :] for u in range(VIEWS_AT_ONCE)]
                for u, later in enumerate(loaded):
                    ahead = flux(later - current)
                    outward = flux(pltpu.roll(current, reach - 1, 1) - current)
                    inward = pltpu.roll(outward, 1, 1)
                    updated = current + ((ahead - before) + (outward - inward))
                    if step < STEPS:
                        field[v + u, rs, :] = updated
                    else:
                        out_ref[v + u - d, rs, :] = updated[:, :width] * (1.0 / SCALE)
                    current, before = later, ahead
                return current, before

            current = field[step, rs, :]
            before = flux(current - field[step - 1, rs, :])
            groups = pl.cdiv(views + 2 * (d - step), VIEWS_AT_ONCE)
            lax.fori_loop(0, groups, some, (current, before))


def per_device(projections, margin, ramp_length):
    views, rows, width = projections.shape
    margin = jnp.broadcast_to(margin[:, None], (rows, LANES))
    ramp = jnp.broadcast_to(ramp_length[:, None], (rows, LANES))
    tall = views + 2 * STEPS
    reach = width + LANES
    f32 = jnp.float32
    shape = jax.ShapeDtypeStruct
    vmem = pl.BlockSpec(memory_space=pltpu.VMEM)
    anywhere = pl.BlockSpec(memory_space=pl.ANY)
    row, band, rim = pl.pallas_call(
        align_kernel,
        out_shape=(
            shape((views, rows, reach), f32),
            shape((views, rows, BAND), f32),
            shape((views, 1, LANES), f32),
        ),
        in_specs=[vmem] * 2,
        out_specs=(vmem,) * 3,
        compiler_params=pltpu.CompilerParams(vmem_limit_bytes=VMEM_LIMIT),
    )(margin, projections)
    parts = pl.pallas_call(
        exchange_kernel,
        out_shape=(
            shape((STEPS, rows, reach), f32),
            shape((STEPS, rows, reach), f32),
            shape((tall, rows, BAND), f32),
            shape((tall, rows, LANES), f32),
            shape((tall, 1, LANES), f32),
            shape((tall, 1, LANES), f32),
        ),
        in_specs=[anywhere] * 3,
        out_specs=(anywhere,) * 6,
        scratch_shapes=[pltpu.SemaphoreType.DMA((16,)), pltpu.SemaphoreType.DMA((16,))],
        compiler_params=pltpu.CompilerParams(collective_id=0, has_side_effects=True),
    )(row, band, rim)
    return pl.pallas_call(
        diffuse_kernel,
        out_shape=shape((views, rows, width), f32),
        in_specs=[vmem] * 9,
        out_specs=vmem,
        scratch_shapes=[pltpu.VMEM((tall + VIEWS_AT_ONCE + 1, rows, reach), f32)],
        compiler_params=pltpu.CompilerParams(vmem_limit_bytes=VMEM_LIMIT),
    )(margin, ramp, row, *parts)


def solution(mesh):
    in_specs = (P("ang", None, "col"), P(), P())
    out_specs = P("ang", None, "col")
    return jax.shard_map(
        per_device, mesh=mesh, in_specs=in_specs, out_specs=out_specs, check_vma=False
    )
```

```python
import functools

import jax
import jax.numpy as jnp
from jax import lax
from jax.experimental import pallas as pl
from jax.experimental.pallas import tpu as pltpu
from jax.sharding import PartitionSpec as P

BAND = 384
STEPS = 6
LANES = 128
BAND_BLOCKS = BAND // LANES
TIME_STEP = 0.2
EDGE_SCALE = 0.8
SCALE = (1.0 / TIME_STEP) ** 0.5 / EDGE_SCALE
MESH = pl.DeviceIdType.MESH
VMEM_LIMIT = 56 * 1024 * 1024
VIEWS_AT_ONCE = 4
ROWS_AT_ONCE = 16
UNROLL = 4


def take_lanes(block, index):
    return jnp.take_along_axis(block, index, axis=1)


def align_kernel(margin_ref, data_ref, row_ref, band_ref, rim_ref):
    views, rows, width = data_ref.shape
    count = width // LANES
    is_last = lax.axis_index("col") == lax.axis_size("col") - 1
    lane = lax.broadcasted_iota(jnp.int32, (8, LANES), 1)
    sublane = lax.broadcasted_iota(jnp.int32, (8, LANES), 0)
    limit = jnp.where(is_last, width, 2 * width)

    def one_view(v, _):
        rim = jnp.zeros((8, LANES), jnp.float32)
        for h in range(rows // 8):
            rs = pl.ds(8 * h, 8)
            margin = margin_ref[rs, :]
            turn = (lane + margin) & (LANES - 1)
            stay = lane + (margin & (LANES - 1)) < LANES
            blocks_on = margin >> 7
            raw = [data_ref[v, rs, pl.ds(LANES * k, LANES)] for k in range(count)]
            turned = [take_lanes(b, turn) for b in raw]
            joined = [jnp.where(stay, turned[k], turned[(k + 1) % count]) for k in range(count)]
            rolled = [
                jnp.where(
                    blocks_on == 1,
                    joined[(k + 1) % count],
                    jnp.where(blocks_on == 2, joined[(k + 2) % count], joined[(k + 3) % count]),
                )
                for k in range(count)
            ]
            edge = take_lanes(raw[-1], jnp.full((8, LANES), LANES - 1, jnp.int32))
            for k in range(count):
                kept = rolled[k]
                if k >= count - BAND_BLOCKS:
                    band_ref[v, rs, pl.ds(LANES * (k - count + BAND_BLOCKS), LANES)] = kept
                    kept = jnp.where(lane + LANES * k + margin < limit, kept, edge)
                row_ref[v, rs, pl.ds(LANES * k, LANES)] = kept
            row_ref[v, rs, pl.ds(width, LANES)] = jnp.where(
                jnp.logical_and(is_last, lane < LANES // 2), edge, rolled[-1]
            )
            head = take_lanes(rolled[0], lane & 7)
            rim = rim + jnp.where((lane >> 3) == sublane + 8 * h, head, 0.0)
        rim_ref[v] = jnp.sum(rim, axis=0, keepdims=True)
        return 0

    lax.fori_loop(0, views, one_view, 0, unroll=UNROLL)


def exchange_kernel(
    row_ref, band_ref, rim_ref,
    low_ref, high_ref, next_ref, mirror_ref, right_ref, facing_ref,
    send_sem, recv_sem,
):
    views = row_ref.shape[0]
    ang, col = lax.axis_index("ang"), lax.axis_index("col")
    n_ang, n_col = lax.axis_size("ang"), lax.axis_size("col")
    half = n_ang // 2
    d = STEPS
    up, down = lax.rem(ang + 1, n_ang), lax.rem(ang + n_ang - 1, n_ang)
    across = lax.rem(ang + half, n_ang)
    across_up, across_down = lax.rem(ang + half + 1, n_ang), lax.rem(ang + half - 1, n_ang)
    prev = jnp.maximum(col - 1, 0)
    after = jnp.minimum(col + 1, n_col - 1)
    has_prev, has_next, at_axis = col > 0, col < n_col - 1, col == 0

    barrier = pltpu.get_barrier_semaphore()

    def greet(a, c):
        pl.semaphore_signal(barrier, inc=1, device_id=(a, c), device_id_type=MESH)

    greet(up, col)
    greet(down, col)

    @pl.when(has_prev)
    def _():
        for a in (ang, up, down):
            greet(a, prev)

    @pl.when(has_next)
    def _():
        for a in (ang, up, down):
            greet(a, after)

    @pl.when(at_axis)
    def _():
        for a in (across, across_up, across_down):
            greet(a, col)

    peers = 2
    for present in (has_prev, has_next, at_axis):
        peers = peers + 3 * present.astype(jnp.int32)
    pl.semaphore_wait(barrier, peers)

    used = [0]

    def copy(src, dst, a, c):
        i = used[0]
        used[0] += 1
        return pltpu.make_async_remote_copy(
            src_ref=src, dst_ref=dst, send_sem=send_sem.at[i], recv_sem=recv_sem.at[i],
            device_id=(a, c), device_id_type=MESH,
        )

    first, last, whole = pl.ds(0, d), pl.ds(views - d, d), pl.ds(0, views)
    low_end, high_end, middle = pl.ds(0, d), pl.ds(views + d, d), pl.ds(d, views)
    tail = pl.ds(BAND - LANES, LANES)

    band_edges = [
        copy(band_ref.at[first], next_ref.at[pl.ds(d, d)], ang, prev),
        copy(band_ref.at[last], next_ref.at[pl.ds(views, d)], ang, prev),
    ]
    inner = views - 2 * d
    band_inner = [copy(band_ref.at[pl.ds(d, inner)], next_ref.at[pl.ds(2 * d, inner)], ang, prev)]
    rims = [
        copy(rim_ref.at[whole], right_ref.at[middle], ang, prev),
        copy(rim_ref.at[first], right_ref.at[high_end], down, prev),
        copy(rim_ref.at[last], right_ref.at[low_end], up, prev),
    ]
    mirrors = [
        copy(rim_ref.at[whole], facing_ref.at[middle], across, col),
        copy(rim_ref.at[first], facing_ref.at[high_end], across_down, col),
        copy(rim_ref.at[last], facing_ref.at[low_end], across_up, col),
        copy(band_ref.at[first, :, tail], mirror_ref.at[high_end], across_down, col),
        copy(band_ref.at[last, :, tail], mirror_ref.at[low_end], across_up, col),
        copy(band_ref.at[whole, :, tail], mirror_ref.at[middle], across, col),
    ]
    turns = [
        copy(row_ref.at[first], high_ref, down, col),
        copy(row_ref.at[last], low_ref, up, col),
    ]
    passed_on = [
        copy(next_ref.at[pl.ds(d, d)], next_ref.at[high_end], down, col),
        copy(next_ref.at[pl.ds(views, d)], next_ref.at[low_end], up, col),
    ]
    leftward = band_edges + rims + band_inner

    @pl.when(has_prev)
    def _():
        for c in leftward:
            c.start()

    @pl.when(at_axis)
    def _():
        for c in mirrors:
            c.start()

    for c in turns:
        c.start()

    @pl.when(has_next)
    def _():
        for c in band_edges:
            c.wait_recv()
        for c in passed_on:
            c.start()
        for c in rims + band_inner:
            c.wait_recv()
        for c in passed_on:
            c.wait()

    @pl.when(at_axis)
    def _():
        for c in mirrors:
            c.wait()

    for c in turns:
        c.wait()

    @pl.when(has_prev)
    def _():
        for c in leftward:
            c.wait_send()


def flux(delta):
    return delta * pl.reciprocal(5.0 + delta * delta, approx=True)


def diffuse_kernel(
    margin_ref, ramp_ref, row_ref, low_ref, high_ref, next_ref, mirror_ref, right_ref, facing_ref,
    out_ref, field,
):
    views, rows, reach = row_ref.shape
    width = reach - LANES
    count = width // LANES
    d = STEPS
    is_last = lax.axis_index("col") == lax.axis_size("col") - 1
    is_first = lax.axis_index("col") == 0
    lane = lax.broadcasted_iota(jnp.int32, (8, LANES), 1)
    sublane = lax.broadcasted_iota(jnp.int32, (8, LANES), 0)
    limit = jnp.where(is_last, 4 * width, width)

    def weight_of(position, spread):
        return jnp.clip(0.5 + (position.astype(jnp.float32) + 0.5) / spread, 0.0, 1.0)

    def stitch(source_ref, offset, length, h):
        rs = pl.ds(8 * h, 8)
        margin = margin_ref[rs, :]
        spread = 2.0 * ramp_ref[rs, :].astype(jnp.float32)
        head = weight_of(lane, spread)
        inner = weight_of(lane - LANES, spread)
        cell = (sublane + 8 * h) * 8

        def one(i, _):
            p = i + offset
            for k in range(1, count):
                block = source_ref[i, rs, pl.ds(LANES * k, LANES)]
                j = k - count + BAND_BLOCKS
                if j >= 0:
                    following = next_ref[p, rs, pl.ds(LANES * j, LANES)]
                    block = jnp.where(lane + LANES * k + margin < limit, block, following)
                field[p, rs, pl.ds(LANES * k, LANES)] = SCALE * block
            block = source_ref[i, rs, pl.ds(0, LANES)]
            facing = take_lanes(mirror_ref[p, rs, :], LANES - 1 - lane)
            blended = head * block + (1.0 - head) * facing
            field[p, rs, pl.ds(0, LANES)] = SCALE * jnp.where(is_first, blended, block)
            block = source_ref[i, rs, pl.ds(width, LANES)]
            facing = take_lanes(jnp.broadcast_to(facing_ref[p], (8, LANES)), cell + ((LANES - 1 - lane) & 7))
            blended = inner * block + (1.0 - inner) * facing
            inward = jnp.where(is_first, blended, block)
            outward = take_lanes(jnp.broadcast_to(right_ref[p], (8, LANES)), cell + (lane & 7))
            outward = jnp.where(is_last, block, outward)
            field[p, rs, pl.ds(width, LANES)] = SCALE * jnp.where(lane < LANES // 2, outward, inward)
            return 0

        lax.fori_loop(0, length, one, 0, unroll=8 if length % 8 == 0 else 6)

    for h in range(rows // 8):
        stitch(low_ref, 0, d, h)
        stitch(row_ref, d, views, h)
        stitch(high_ref, views + d, d, h)

    slabs = range(0, rows, ROWS_AT_ONCE)
    for step in range(1, STEPS + 1):
        for first_row in slabs:
            rs = pl.ds(first_row, ROWS_AT_ONCE)

            def some(i, carried):
                current, before = carried
                v = step + i * VIEWS_AT_ONCE
                loaded = [field[v + 1 + u, rs, :] for u in range(VIEWS_AT_ONCE)]
                for u, later in enumerate(loaded):
                    ahead = flux(later - current)
                    outward = flux(pltpu.roll(current, reach - 1, 1) - current)
                    inward = pltpu.roll(outward, 1, 1)
                    updated = current + ((ahead - before) + (outward - inward))
                    if step < STEPS:
                        field[v + u, rs, :] = updated
                    else:
                        out_ref[v + u - d, rs, :] = updated[:, :width] * (1.0 / SCALE)
                    current, before = later, ahead
                return current, before

            current = field[step, rs, :]
            before = flux(current - field[step - 1, rs, :])
            groups = pl.cdiv(views + 2 * (d - step), VIEWS_AT_ONCE)
            lax.fori_loop(0, groups, some, (current, before))


def per_device(projections, margin, ramp_length):
    views, rows, width = projections.shape
    margin = jnp.broadcast_to(margin[:, None], (rows, LANES))
    ramp = jnp.broadcast_to(ramp_length[:, None], (rows, LANES))
    tall = views + 2 * STEPS
    reach = width + LANES
    f32 = jnp.float32
    shape = jax.ShapeDtypeStruct
    vmem = pl.BlockSpec(memory_space=pltpu.VMEM)
    anywhere = pl.BlockSpec(memory_space=pl.ANY)
    row, band, rim = pl.pallas_call(
        align_kernel,
        out_shape=(
            shape((views, rows, reach), f32),
            shape((views, rows, BAND), f32),
            shape((views, 1, LANES), f32),
        ),
        in_specs=[vmem] * 2,
        out_specs=(vmem,) * 3,
        compiler_params=pltpu.CompilerParams(vmem_limit_bytes=VMEM_LIMIT),
    )(margin, projections)
    parts = pl.pallas_call(
        exchange_kernel,
        out_shape=(
            shape((STEPS, rows, reach), f32),
            shape((STEPS, rows, reach), f32),
            shape((tall, rows, BAND), f32),
            shape((tall, rows, LANES), f32),
            shape((tall, 1, LANES), f32),
            shape((tall, 1, LANES), f32),
        ),
        in_specs=[anywhere] * 3,
        out_specs=(anywhere,) * 6,
        scratch_shapes=[pltpu.SemaphoreType.DMA((16,)), pltpu.SemaphoreType.DMA((16,))],
        compiler_params=pltpu.CompilerParams(collective_id=0, has_side_effects=True),
    )(row, band, rim)
    return pl.pallas_call(
        diffuse_kernel,
        out_shape=shape((views, rows, width), f32),
        in_specs=[vmem] * 9,
        out_specs=vmem,
        scratch_shapes=[pltpu.VMEM((tall + VIEWS_AT_ONCE + 1, rows, reach), f32)],
        compiler_params=pltpu.CompilerParams(vmem_limit_bytes=VMEM_LIMIT),
    )(margin, ramp, row, *parts)


def solution(mesh):
    in_specs = (P("ang", None, "col"), P(), P())
    out_specs = P("ang", None, "col")
    return jax.shard_map(
        per_device, mesh=mesh, in_specs=in_specs, out_specs=out_specs, check_vma=False
    )
```

```python
import functools

import jax
import jax.numpy as jnp
from jax import lax
from jax.experimental import pallas as pl
from jax.experimental.pallas import tpu as pltpu
from jax.sharding import PartitionSpec as P

BAND = 384
STEPS = 6
LANES = 128
BAND_BLOCKS = BAND // LANES
TIME_STEP = 0.2
EDGE_SCALE = 0.8
SCALE = (1.0 / TIME_STEP) ** 0.5 / EDGE_SCALE
MESH = pl.DeviceIdType.MESH
VMEM_LIMIT = 56 * 1024 * 1024
VIEWS_AT_ONCE = 4
ROWS_AT_ONCE = 16
UNROLL = 4


def take_lanes(block, index):
    return jnp.take_along_axis(block, index, axis=1)


def align_kernel(margin_ref, data_ref, row_ref, band_ref, rim_ref):
    views, rows, width = data_ref.shape
    count = width // LANES
    is_last = lax.axis_index("col") == lax.axis_size("col") - 1
    lane = lax.broadcasted_iota(jnp.int32, (8, LANES), 1)
    sublane = lax.broadcasted_iota(jnp.int32, (8, LANES), 0)
    limit = jnp.where(is_last, width, 2 * width)

    def one_view(v, _):
        rim = jnp.zeros((8, LANES), jnp.float32)
        for h in range(rows // 8):
            rs = pl.ds(8 * h, 8)
            margin = jnp.broadcast_to(margin_ref[rs, :], (8, LANES))
            turn = (lane + margin) & (LANES - 1)
            stay = lane + (margin & (LANES - 1)) < LANES
            blocks_on = margin >> 7
            raw = [data_ref[v, rs, pl.ds(LANES * k, LANES)] for k in range(count)]
            turned = [take_lanes(b, turn) for b in raw]
            joined = [jnp.where(stay, turned[k], turned[(k + 1) % count]) for k in range(count)]
            rolled = [
                jnp.where(
                    blocks_on == 1,
                    joined[(k + 1) % count],
                    jnp.where(blocks_on == 2, joined[(k + 2) % count], joined[(k + 3) % count]),
                )
                for k in range(count)
            ]
            edge = take_lanes(raw[-1], jnp.full((8, LANES), LANES - 1, jnp.int32))
            for k in range(count):
                kept = rolled[k]
                if k >= count - BAND_BLOCKS:
                    band_ref[v, rs, pl.ds(LANES * (k - count + BAND_BLOCKS), LANES)] = kept
                    kept = jnp.where(lane + LANES * k + margin < limit, kept, edge)
                row_ref[v, rs, pl.ds(LANES * k, LANES)] = kept
            row_ref[v, rs, pl.ds(width, LANES)] = jnp.where(
                jnp.logical_and(is_last, lane < LANES // 2), edge, rolled[-1]
            )
            head = take_lanes(rolled[0], lane & 7)
            rim = rim + jnp.where((lane >> 3) == sublane + 8 * h, head, 0.0)
        rim_ref[v] = jnp.sum(rim, axis=0, keepdims=True)
        return 0

    lax.fori_loop(0, views, one_view, 0, unroll=UNROLL)


def exchange_kernel(
    row_ref, band_ref, rim_ref,
    low_ref, high_ref, next_ref, mirror_ref, right_ref, facing_ref,
    send_sem, recv_sem,
):
    views = row_ref.shape[0]
    ang, col = lax.axis_index("ang"), lax.axis_index("col")
    n_ang, n_col = lax.axis_size("ang"), lax.axis_size("col")
    half = n_ang // 2
    d = STEPS
    up, down = lax.rem(ang + 1, n_ang), lax.rem(ang + n_ang - 1, n_ang)
    across = lax.rem(ang + half, n_ang)
    across_up, across_down = lax.rem(ang + half + 1, n_ang), lax.rem(ang + half - 1, n_ang)
    prev = jnp.maximum(col - 1, 0)
    after = jnp.minimum(col + 1, n_col - 1)
    has_prev, has_next, at_axis = col > 0, col < n_col - 1, col == 0

    barrier = pltpu.get_barrier_semaphore()

    def greet(a, c):
        pl.semaphore_signal(barrier, inc=1, device_id=(a, c), device_id_type=MESH)

    greet(up, col)
    greet(down, col)

    @pl.when(has_prev)
    def _():
        for a in (ang, up, down):
            greet(a, prev)

    @pl.when(has_next)
    def _():
        for a in (ang, up, down):
            greet(a, after)

    @pl.when(at_axis)
    def _():
        for a in (across, across_up, across_down):
            greet(a, col)

    peers = 2
    for present in (has_prev, has_next, at_axis):
        peers = peers + 3 * present.astype(jnp.int32)
    pl.semaphore_wait(barrier, peers)

    used = [0]

    def copy(src, dst, a, c):
        i = used[0]
        used[0] += 1
        return pltpu.make_async_remote_copy(
            src_ref=src, dst_ref=dst, send_sem=send_sem.at[i], recv_sem=recv_sem.at[i],
            device_id=(a, c), device_id_type=MESH,
        )

    first, last, whole = pl.ds(0, d), pl.ds(views - d, d), pl.ds(0, views)
    low_end, high_end, middle = pl.ds(0, d), pl.ds(views + d, d), pl.ds(d, views)
    tail = pl.ds(BAND - LANES, LANES)

    band_edges = [
        copy(band_ref.at[first], next_ref.at[pl.ds(d, d)], ang, prev),
        copy(band_ref.at[last], next_ref.at[pl.ds(views, d)], ang, prev),
    ]
    inner = views - 2 * d
    band_inner = [copy(band_ref.at[pl.ds(d, inner)], next_ref.at[pl.ds(2 * d, inner)], ang, prev)]
    rims = [
        copy(rim_ref.at[whole], right_ref.at[middle], ang, prev),
        copy(rim_ref.at[first], right_ref.at[high_end], down, prev),
        copy(rim_ref.at[last], right_ref.at[low_end], up, prev),
    ]
    mirrors = [
        copy(rim_ref.at[whole], facing_ref.at[middle], across, col),
        copy(rim_ref.at[first], facing_ref.at[high_end], across_down, col),
        copy(rim_ref.at[last], facing_ref.at[low_end], across_up, col),
        copy(band_ref.at[first, :, tail], mirror_ref.at[high_end], across_down, col),
        copy(band_ref.at[last, :, tail], mirror_ref.at[low_end], across_up, col),
        copy(band_ref.at[whole, :, tail], mirror_ref.at[middle], across, col),
    ]
    turns = [
        copy(row_ref.at[first], high_ref, down, col),
        copy(row_ref.at[last], low_ref, up, col),
    ]
    passed_on = [
        copy(next_ref.at[pl.ds(d, d)], next_ref.at[high_end], down, col),
        copy(next_ref.at[pl.ds(views, d)], next_ref.at[low_end], up, col),
    ]
    leftward = band_edges + rims + band_inner

    @pl.when(has_prev)
    def _():
        for c in leftward:
            c.start()

    @pl.when(at_axis)
    def _():
        for c in mirrors:
            c.start()

    for c in turns:
        c.start()

    @pl.when(has_next)
    def _():
        for c in band_edges:
            c.wait_recv()
        for c in passed_on:
            c.start()
        for c in rims + band_inner:
            c.wait_recv()
        for c in passed_on:
            c.wait()

    @pl.when(at_axis)
    def _():
        for c in mirrors:
            c.wait()

    for c in turns:
        c.wait()

    @pl.when(has_prev)
    def _():
        for c in leftward:
            c.wait_send()


def flux(delta):
    return delta * pl.reciprocal(5.0 + delta * delta, approx=True)


def diffuse_kernel(
    margin_ref, ramp_ref, row_ref, low_ref, high_ref, next_ref, mirror_ref, right_ref, facing_ref,
    out_ref, field,
):
    views, rows, reach = row_ref.shape
    width = reach - LANES
    count = width // LANES
    d = STEPS
    is_last = lax.axis_index("col") == lax.axis_size("col") - 1
    is_first = lax.axis_index("col") == 0
    lane = lax.broadcasted_iota(jnp.int32, (8, LANES), 1)
    sublane = lax.broadcasted_iota(jnp.int32, (8, LANES), 0)
    limit = jnp.where(is_last, 4 * width, width)

    def weight_of(position, spread):
        return jnp.clip(0.5 + (position.astype(jnp.float32) + 0.5) / spread, 0.0, 1.0)

    def stitch(source_ref, offset, length, h):
        rs = pl.ds(8 * h, 8)
        margin = jnp.broadcast_to(margin_ref[rs, :], (8, LANES))
        spread = 2.0 * jnp.broadcast_to(ramp_ref[rs, :], (8, LANES)).astype(jnp.float32)
        head = weight_of(lane, spread)
        inner = weight_of(lane - LANES, spread)
        cell = (sublane + 8 * h) * 8

        def one(i, _):
            p = i + offset
            for k in range(1, count):
                block = source_ref[i, rs, pl.ds(LANES * k, LANES)]
                j = k - count + BAND_BLOCKS
                if j >= 0:
                    following = next_ref[p, rs, pl.ds(LANES * j, LANES)]
                    block = jnp.where(lane + LANES * k + margin < limit, block, following)
                field[p, rs, pl.ds(LANES * k, LANES)] = SCALE * block
            block = source_ref[i, rs, pl.ds(0, LANES)]
            facing = take_lanes(mirror_ref[p, rs, :], LANES - 1 - lane)
            blended = head * block + (1.0 - head) * facing
            field[p, rs, pl.ds(0, LANES)] = SCALE * jnp.where(is_first, blended, block)
            block = source_ref[i, rs, pl.ds(width, LANES)]
            facing = take_lanes(jnp.broadcast_to(facing_ref[p], (8, LANES)), cell + ((LANES - 1 - lane) & 7))
            blended = inner * block + (1.0 - inner) * facing
            inward = jnp.where(is_first, blended, block)
            outward = take_lanes(jnp.broadcast_to(right_ref[p], (8, LANES)), cell + (lane & 7))
            outward = jnp.where(is_last, block, outward)
            field[p, rs, pl.ds(width, LANES)] = SCALE * jnp.where(lane < LANES // 2, outward, inward)
            return 0

        lax.fori_loop(0, length, one, 0, unroll=8 if length % 8 == 0 else 6)

    for h in range(rows // 8):
        stitch(low_ref, 0, d, h)
        stitch(row_ref, d, views, h)
        stitch(high_ref, views + d, d, h)

    slabs = range(0, rows, ROWS_AT_ONCE)
    for step in range(1, STEPS + 1):
        for first_row in slabs:
            rs = pl.ds(first_row, ROWS_AT_ONCE)

            def some(i, carried):
                current, before = carried
                v = step + i * VIEWS_AT_ONCE
                loaded = [field[v + 1 + u, rs, :] for u in range(VIEWS_AT_ONCE)]
                for u, later in enumerate(loaded):
                    ahead = flux(later - current)
                    outward = flux(pltpu.roll(current, reach - 1, 1) - current)
                    inward = pltpu.roll(outward, 1, 1)
                    updated = current + ((ahead - before) + (outward - inward))
                    if step < STEPS:
                        field[v + u, rs, :] = updated
                    else:
                        out_ref[v + u - d, rs, :] = updated[:, :width] * (1.0 / SCALE)
                    current, before = later, ahead
                return current, before

            current = field[step, rs, :]
            before = flux(current - field[step - 1, rs, :])
            groups = pl.cdiv(views + 2 * (d - step), VIEWS_AT_ONCE)
            lax.fori_loop(0, groups, some, (current, before))


def per_device(projections, margin, ramp_length):
    views, rows, width = projections.shape
    margin = margin[:, None]
    ramp = ramp_length[:, None]
    tall = views + 2 * STEPS
    reach = width + LANES
    f32 = jnp.float32
    shape = jax.ShapeDtypeStruct
    vmem = pl.BlockSpec(memory_space=pltpu.VMEM)
    anywhere = pl.BlockSpec(memory_space=pl.ANY)
    row, band, rim = pl.pallas_call(
        align_kernel,
        out_shape=(
            shape((views, rows, reach), f32),
            shape((views, rows, BAND), f32),
            shape((views, 1, LANES), f32),
        ),
        in_specs=[vmem] * 2,
        out_specs=(vmem,) * 3,
        compiler_params=pltpu.CompilerParams(vmem_limit_bytes=VMEM_LIMIT),
    )(margin, projections)
    parts = pl.pallas_call(
        exchange_kernel,
        out_shape=(
            shape((STEPS, rows, reach), f32),
            shape((STEPS, rows, reach), f32),
            shape((tall, rows, BAND), f32),
            shape((tall, rows, LANES), f32),
            shape((tall, 1, LANES), f32),
            shape((tall, 1, LANES), f32),
        ),
        in_specs=[anywhere] * 3,
        out_specs=(anywhere,) * 6,
        scratch_shapes=[pltpu.SemaphoreType.DMA((16,)), pltpu.SemaphoreType.DMA((16,))],
        compiler_params=pltpu.CompilerParams(collective_id=0, has_side_effects=True),
    )(row, band, rim)
    return pl.pallas_call(
        diffuse_kernel,
        out_shape=shape((views, rows, width), f32),
        in_specs=[vmem] * 9,
        out_specs=vmem,
        scratch_shapes=[pltpu.VMEM((tall + VIEWS_AT_ONCE + 1, rows, reach), f32)],
        compiler_params=pltpu.CompilerParams(vmem_limit_bytes=VMEM_LIMIT),
    )(margin, ramp, row, *parts)


def solution(mesh):
    in_specs = (P("ang", None, "col"), P(), P())
    out_specs = P("ang", None, "col")
    return jax.shard_map(
        per_device, mesh=mesh, in_specs=in_specs, out_specs=out_specs, check_vma=False
    )
```

```python
import functools

import jax
import jax.numpy as jnp
from jax import lax
from jax.experimental import pallas as pl
from jax.experimental.pallas import tpu as pltpu
from jax.sharding import PartitionSpec as P

BAND = 384
STEPS = 6
LANES = 128
BAND_BLOCKS = BAND // LANES
TIME_STEP = 0.2
EDGE_SCALE = 0.8
SCALE = (1.0 / TIME_STEP) ** 0.5 / EDGE_SCALE
MESH = pl.DeviceIdType.MESH
VMEM_LIMIT = 56 * 1024 * 1024
VIEWS_AT_ONCE = 4
ROWS_AT_ONCE = 16
UNROLL = 4


def take_lanes(block, index):
    return jnp.take_along_axis(block, index, axis=1)


def align_kernel(margin_ref, data_ref, row_ref, band_ref, rim_ref):
    views, rows, width = data_ref.shape
    count = width // LANES
    is_last = lax.axis_index("col") == lax.axis_size("col") - 1
    lane = lax.broadcasted_iota(jnp.int32, (8, LANES), 1)
    sublane = lax.broadcasted_iota(jnp.int32, (8, LANES), 0)
    limit = jnp.where(is_last, width, 2 * width)

    def one_view(v, _):
        rim = jnp.zeros((8, LANES), jnp.float32)
        for h in range(rows // 8):
            rs = pl.ds(8 * h, 8)
            margin = margin_ref[rs, :]
            turn = (lane + margin) & (LANES - 1)
            stay = lane + (margin & (LANES - 1)) < LANES
            blocks_on = margin >> 7
            raw = [data_ref[v, rs, pl.ds(LANES * k, LANES)] for k in range(count)]
            turned = [take_lanes(b, turn) for b in raw]
            joined = [jnp.where(stay, turned[k], turned[(k + 1) % count]) for k in range(count)]
            rolled = [
                jnp.where(
                    blocks_on == 1,
                    joined[(k + 1) % count],
                    jnp.where(blocks_on == 2, joined[(k + 2) % count], joined[(k + 3) % count]),
                )
                for k in range(count)
            ]
            edge = take_lanes(raw[-1], jnp.full((8, LANES), LANES - 1, jnp.int32))
            for k in range(count):
                kept = rolled[k]
                if k >= count - BAND_BLOCKS:
                    band_ref[v, rs, pl.ds(LANES * (k - count + BAND_BLOCKS), LANES)] = kept
                    kept = jnp.where(lane + LANES * k + margin < limit, kept, edge)
                row_ref[v, rs, pl.ds(LANES * k, LANES)] = kept
            row_ref[v, rs, pl.ds(width, LANES)] = jnp.where(
                jnp.logical_and(is_last, lane < LANES // 2), edge, rolled[-1]
            )
            head = take_lanes(rolled[0], lane & 7)
            rim = rim + jnp.where((lane >> 3) == sublane + 8 * h, head, 0.0)
        rim_ref[v] = jnp.sum(rim, axis=0, keepdims=True)
        return 0

    lax.fori_loop(0, views, one_view, 0, unroll=UNROLL)


def exchange_kernel(
    row_ref, band_ref, rim_ref,
    low_ref, high_ref, next_ref, mirror_ref, right_ref, facing_ref,
    send_sem, recv_sem,
):
    views = row_ref.shape[0]
    ang, col = lax.axis_index("ang"), lax.axis_index("col")
    n_ang, n_col = lax.axis_size("ang"), lax.axis_size("col")
    half = n_ang // 2
    d = STEPS
    up, down = lax.rem(ang + 1, n_ang), lax.rem(ang + n_ang - 1, n_ang)
    across = lax.rem(ang + half, n_ang)
    across_up, across_down = lax.rem(ang + half + 1, n_ang), lax.rem(ang + half - 1, n_ang)
    prev = jnp.maximum(col - 1, 0)
    after = jnp.minimum(col + 1, n_col - 1)
    has_prev, has_next, at_axis = col > 0, col < n_col - 1, col == 0

    barrier = pltpu.get_barrier_semaphore()

    def greet(a, c):
        pl.semaphore_signal(barrier, inc=1, device_id=(a, c), device_id_type=MESH)

    greet(up, col)
    greet(down, col)

    @pl.when(has_prev)
    def _():
        for a in (ang, up, down):
            greet(a, prev)

    @pl.when(has_next)
    def _():
        for a in (ang, up, down):
            greet(a, after)

    @pl.when(at_axis)
    def _():
        for a in (across, across_up, across_down):
            greet(a, col)

    peers = 2
    for present in (has_prev, has_next, at_axis):
        peers = peers + 3 * present.astype(jnp.int32)
    pl.semaphore_wait(barrier, peers)

    used = [0]

    def copy(src, dst, a, c):
        i = used[0]
        used[0] += 1
        return pltpu.make_async_remote_copy(
            src_ref=src, dst_ref=dst, send_sem=send_sem.at[i], recv_sem=recv_sem.at[i],
            device_id=(a, c), device_id_type=MESH,
        )

    first, last, whole = pl.ds(0, d), pl.ds(views - d, d), pl.ds(0, views)
    low_end, high_end, middle = pl.ds(0, d), pl.ds(views + d, d), pl.ds(d, views)
    tail = pl.ds(BAND - LANES, LANES)

    band_edges = [
        copy(band_ref.at[first], next_ref.at[pl.ds(d, d)], ang, prev),
        copy(band_ref.at[last], next_ref.at[pl.ds(views, d)], ang, prev),
    ]
    inner = views - 2 * d
    band_inner = [copy(band_ref.at[pl.ds(d, inner)], next_ref.at[pl.ds(2 * d, inner)], ang, prev)]
    rims = [
        copy(rim_ref.at[whole], right_ref.at[middle], ang, prev),
        copy(rim_ref.at[first], right_ref.at[high_end], down, prev),
        copy(rim_ref.at[last], right_ref.at[low_end], up, prev),
    ]
    mirrors = [
        copy(rim_ref.at[whole], facing_ref.at[middle], across, col),
        copy(rim_ref.at[first], facing_ref.at[high_end], across_down, col),
        copy(rim_ref.at[last], facing_ref.at[low_end], across_up, col),
        copy(band_ref.at[first, :, tail], mirror_ref.at[high_end], across_down, col),
        copy(band_ref.at[last, :, tail], mirror_ref.at[low_end], across_up, col),
        copy(band_ref.at[whole, :, tail], mirror_ref.at[middle], across, col),
    ]
    turns = [
        copy(row_ref.at[first], high_ref, down, col),
        copy(row_ref.at[last], low_ref, up, col),
    ]
    passed_on = [
        copy(next_ref.at[pl.ds(d, d)], next_ref.at[high_end], down, col),
        copy(next_ref.at[pl.ds(views, d)], next_ref.at[low_end], up, col),
    ]
    leftward = band_edges + rims + band_inner

    @pl.when(has_prev)
    def _():
        for c in leftward:
            c.start()

    @pl.when(at_axis)
    def _():
        for c in mirrors:
            c.start()

    for c in turns:
        c.start()

    @pl.when(has_next)
    def _():
        for c in band_edges:
            c.wait_recv()
        for c in passed_on:
            c.start()
        for c in rims + band_inner:
            c.wait_recv()
        for c in passed_on:
            c.wait()

    @pl.when(at_axis)
    def _():
        for c in mirrors:
            c.wait()

    for c in turns:
        c.wait()

    @pl.when(has_prev)
    def _():
        for c in leftward:
            c.wait_send()


def flux(delta):
    return delta * pl.reciprocal(5.0 + delta * delta, approx=True)


def diffuse_kernel(
    margin_ref, ramp_ref, row_ref, low_ref, high_ref, next_ref, mirror_ref, right_ref, facing_ref,
    out_ref, field,
):
    views, rows, reach = row_ref.shape
    width = reach - LANES
    count = width // LANES
    d = STEPS
    is_last = lax.axis_index("col") == lax.axis_size("col") - 1
    is_first = lax.axis_index("col") == 0
    lane = lax.broadcasted_iota(jnp.int32, (8, LANES), 1)
    sublane = lax.broadcasted_iota(jnp.int32, (8, LANES), 0)
    limit = jnp.where(is_last, 4 * width, width)

    def weight_of(position, spread):
        return jnp.clip(0.5 + (position.astype(jnp.float32) + 0.5) / spread, 0.0, 1.0)

    def stitch(source_ref, offset, length, h):
        rs = pl.ds(8 * h, 8)
        margin = margin_ref[rs, :]
        spread = 2.0 * ramp_ref[rs, :].astype(jnp.float32)
        head = weight_of(lane, spread)
        inner = weight_of(lane - LANES, spread)
        cell = (sublane + 8 * h) * 8

        def one(i, _):
            p = i + offset
            for k in range(1, count):
                block = source_ref[i, rs, pl.ds(LANES * k, LANES)]
                j = k - count + BAND_BLOCKS
                if j >= 0:
                    following = next_ref[p, rs, pl.ds(LANES * j, LANES)]
                    block = jnp.where(lane + LANES * k + margin < limit, block, following)
                field[p, rs, pl.ds(LANES * k, LANES)] = SCALE * block
            block = source_ref[i, rs, pl.ds(0, LANES)]
            facing = take_lanes(mirror_ref[p, rs, :], LANES - 1 - lane)
            blended = head * block + (1.0 - head) * facing
            field[p, rs, pl.ds(0, LANES)] = SCALE * jnp.where(is_first, blended, block)
            block = source_ref[i, rs, pl.ds(width, LANES)]
            facing = take_lanes(jnp.broadcast_to(facing_ref[p], (8, LANES)), cell + ((LANES - 1 - lane) & 7))
            blended = inner * block + (1.0 - inner) * facing
            inward = jnp.where(is_first, blended, block)
            outward = take_lanes(jnp.broadcast_to(right_ref[p], (8, LANES)), cell + (lane & 7))
            outward = jnp.where(is_last, block, outward)
            field[p, rs, pl.ds(width, LANES)] = SCALE * jnp.where(lane < LANES // 2, outward, inward)
            return 0

        lax.fori_loop(0, length, one, 0, unroll=8 if length % 8 == 0 else 6)

    for h in range(rows // 8):
        stitch(low_ref, 0, d, h)
        stitch(row_ref, d, views, h)
        stitch(high_ref, views + d, d, h)

    slabs = range(0, rows, ROWS_AT_ONCE)
    for step in range(1, STEPS + 1):
        for first_row in slabs:
            rs = pl.ds(first_row, ROWS_AT_ONCE)

            def some(i, carried):
                current, before = carried
                v = step + i * VIEWS_AT_ONCE
                for u in range(VIEWS_AT_ONCE):
                    later = field[v + 1 + u, rs, :]
                    ahead = flux(later - current)
                    outward = flux(pltpu.roll(current, reach - 1, 1) - current)
                    inward = pltpu.roll(outward, 1, 1)
                    updated = current + ((ahead - before) + (outward - inward))
                    if step < STEPS:
                        field[v + u, rs, :] = updated
                    else:
                        out_ref[v + u - d, rs, :] = updated[:, :width] * (1.0 / SCALE)
                    current, before = later, ahead
                return current, before

            current = field[step, rs, :]
            before = flux(current - field[step - 1, rs, :])
            groups = pl.cdiv(views + 2 * (d - step), VIEWS_AT_ONCE)
            lax.fori_loop(0, groups, some, (current, before))


def per_device(projections, margin, ramp_length):
    views, rows, width = projections.shape
    margin = jnp.broadcast_to(margin[:, None], (rows, LANES))
    ramp = jnp.broadcast_to(ramp_length[:, None], (rows, LANES))
    tall = views + 2 * STEPS
    reach = width + LANES
    chunk = 32
    f32 = jnp.float32
    shape = jax.ShapeDtypeStruct
    vmem = pl.BlockSpec(memory_space=pltpu.VMEM)
    anywhere = pl.BlockSpec(memory_space=pl.ANY)
    row, band, rim = pl.pallas_call(
        align_kernel,
        out_shape=(
            shape((views, rows, reach), f32),
            shape((views, rows, BAND), f32),
            shape((views, 1, LANES), f32),
        ),
        grid=(views // chunk,),
        in_specs=[
            pl.BlockSpec((rows, LANES), lambda i: (0, 0)),
            pl.BlockSpec((chunk, rows, width), lambda i: (i, 0, 0)),
        ],
        out_specs=(
            pl.BlockSpec((chunk, rows, reach), lambda i: (i, 0, 0)),
            pl.BlockSpec((chunk, rows, BAND), lambda i: (i, 0, 0)),
            pl.BlockSpec((chunk, 1, LANES), lambda i: (i, 0, 0)),
        ),
        compiler_params=pltpu.CompilerParams(vmem_limit_bytes=VMEM_LIMIT),
    )(margin, projections)
    parts = pl.pallas_call(
        exchange_kernel,
        out_shape=(
            shape((STEPS, rows, reach), f32),
            shape((STEPS, rows, reach), f32),
            shape((tall, rows, BAND), f32),
            shape((tall, rows, LANES), f32),
            shape((tall, 1, LANES), f32),
            shape((tall, 1, LANES), f32),
        ),
        in_specs=[anywhere] * 3,
        out_specs=(anywhere,) * 6,
        scratch_shapes=[pltpu.SemaphoreType.DMA((16,)), pltpu.SemaphoreType.DMA((16,))],
        compiler_params=pltpu.CompilerParams(collective_id=0, has_side_effects=True),
    )(row, band, rim)
    return pl.pallas_call(
        diffuse_kernel,
        out_shape=shape((views, rows, width), f32),
        in_specs=[vmem] * 9,
        out_specs=vmem,
        scratch_shapes=[pltpu.VMEM((tall + VIEWS_AT_ONCE + 1, rows, reach), f32)],
        compiler_params=pltpu.CompilerParams(vmem_limit_bytes=VMEM_LIMIT),
    )(margin, ramp, row, *parts)


def solution(mesh):
    in_specs = (P("ang", None, "col"), P(), P())
    out_specs = P("ang", None, "col")
    return jax.shard_map(
        per_device, mesh=mesh, in_specs=in_specs, out_specs=out_specs, check_vma=False
    )
```
